32 devices in a mesh: wide: 8 (over z, x), narrow: 4 (over y, core).
Axes of the slice: x: 2, y: 2, z: 4, core: 2. Of those that a mesh axis runs over, the one named last changes fastest.
Arguments:
- block_input: float32 [16384, 1152], P('wide', 'narrow'), may hold values from -6 to 6
- condition: float32 [4, 1152], replicated, may hold values from -6 to 6
- frame_counts: int32 [4], replicated, may hold values from 8 to 16, as said below
- cotangent: float32 [16384, 1152], P('wide', 'narrow'), may hold values from -6 to 6
- qkv_weight: float32 [2, 1152, 3, 1152], P(None, 'wide', None, 'narrow'), may hold values from -0.23570226 to 0.23570226
- qkv_first: float32 [2, 1152, 3, 1152], P(None, 'wide', None, 'narrow'), may hold values from -0.00021362305 to 0.00021362305
- qkv_second: float32 [2, 1152, 3, 1152], P(None, 'wide', None, 'narrow'), may hold values from 2.0917e-11 to 8.3668e-11
- out_weight: float32 [2, 1152, 1152], P(None, 'wide', 'narrow'), may hold values from -0.94280904 to 0.94280904
- out_first: float32 [2, 1152, 1152], P(None, 'wide', 'narrow'), may hold values from -0.00021362305 to 0.00021362305
- out_second: float32 [2, 1152, 1152], P(None, 'wide', 'narrow'), may hold values from 2.0917e-11 to 8.3668e-11
- up_weight: float32 [2, 1152, 4, 1152], P(None, 'wide', None, 'narrow'), may hold values from -0.23570226 to 0.23570226
- up_first: float32 [2, 1152, 4, 1152], P(None, 'wide', None, 'narrow'), may hold values from -0.00021362305 to 0.00021362305
- up_second: float32 [2, 1152, 4, 1152], P(None, 'wide', None, 'narrow'), may hold values from 2.0917e-11 to 8.3668e-11
- down_weight: float32 [2, 1152, 4, 1152], P(None, 'wide', None, 'narrow'), may hold values from -0.11785113 to 0.11785113
- down_first: float32 [2, 1152, 4, 1152], P(None, 'wide', None, 'narrow'), may hold values from -0.00021362305 to 0.00021362305
- down_second: float32 [2, 1152, 4, 1152], P(None, 'wide', None, 'narrow'), may hold values from 2.0917e-11 to 8.3668e-11
- ada_weight: float32 [2, 1152, 6, 1152], P(None, 'wide', None, 'narrow'), may hold values from -0.23570226 to 0.23570226
- ada_first: float32 [2, 1152, 6, 1152], P(None, 'wide', None, 'narrow'), may hold values from -0.00021362305 to 0.00021362305
- ada_second: float32 [2, 1152, 6, 1152], P(None, 'wide', None, 'narrow'), may hold values from 2.0917e-11 to 8.3668e-11
- bias_weight: float32 [2, 14, 1152], P(None, None, 'narrow'), may hold values from -4 to 4
- bias_first: float32 [2, 14, 1152], P(None, None, 'narrow'), may hold values from -0.00061035156 to 0.00061035156
- bias_second: float32 [2, 14, 1152], P(None, None, 'narrow'), may hold values from 2.0917001e-10 to 8.3668006e-10
Outputs:
- block_output: float32 [16384, 1152], P('wide', 'narrow')
- input_grad: float32 [16384, 1152], P('wide', 'narrow')
- qkv_next: float32 [2, 1152, 3, 1152], P(None, 'wide', None, 'narrow')
- qkv_moment: float32 [2, 1152, 3, 1152], P(None, 'wide', None, 'narrow')
- qkv_square: float32 [2, 1152, 3, 1152], P(None, 'wide', None, 'narrow')
- out_next: float32 [2, 1152, 1152], P(None, 'wide', 'narrow')
- out_moment: float32 [2, 1152, 1152], P(None, 'wide', 'narrow')
- out_square: float32 [2, 1152, 1152], P(None, 'wide', 'narrow')
- up_next: float32 [2, 1152, 4, 1152], P(None, 'wide', None, 'narrow')
- up_moment: float32 [2, 1152, 4, 1152], P(None, 'wide', None, 'narrow')
- up_square: float32 [2, 1152, 4, 1152], P(None, 'wide', None, 'narrow')
- down_next: float32 [2, 1152, 4, 1152], P(None, 'wide', None, 'narrow')
- down_moment: float32 [2, 1152, 4, 1152], P(None, 'wide', None, 'narrow')
- down_square: float32 [2, 1152, 4, 1152], P(None, 'wide', None, 'narrow')
- ada_next: float32 [2, 1152, 6, 1152], P(None, 'wide', None, 'narrow')
- ada_moment: float32 [2, 1152, 6, 1152], P(None, 'wide', None, 'narrow')
- ada_square: float32 [2, 1152, 6, 1152], P(None, 'wide', None, 'narrow')
- bias_next: float32 [2, 14, 1152], P(None, None, 'narrow')
- bias_moment: float32 [2, 14, 1152], P(None, None, 'narrow')
- bias_square: float32 [2, 14, 1152], P(None, None, 'narrow')
- trust_norms: float32 [2, 6, 2], replicated
- grad_norm: float32 [1], replicated
The draws below stay inside these ranges and needn't reach their ends.
Inputs may be any that keep to these rules, and one draw needn't show every extreme that they name: Clip c holds frame_counts[c] frames of data at its first positions, the rest of its 16 frames are padding that no token attends to; some clip holds 16 frames.
All inputs are finite; a program needn't handle non-finite values.
Results may differ from the reference program's by a relative error of at most 0.04.
Values may be sent and summed in bfloat16 or wider, within the bound.
A program may use at most 320 MiB of HBM per device.

```python
import math
import jax
import jax.numpy as jnp
from jax import lax

D = 1152
HEADS = 16
HEAD_DIM = 72
FF = 4608
PATCHES = 256
CLIP_LEN = 16
STEP = 10
TOKENS = 16384
CLIPS = 4
BIAS_ROWS = 14
PARAMS = 47808000


def draw_frame_counts(key, part):
    key = jax.random.fold_in(key, 17)
    first_key, second_key = jax.random.split(key, 2)
    counts = jax.random.randint(first_key, (CLIPS,), CLIP_LEN // 2, CLIP_LEN + 1)
    longest = jax.random.randint(second_key, (), 0, CLIPS)
    positions = jnp.arange(CLIPS, dtype=jnp.int32)
    counts = jnp.where(positions == longest, CLIP_LEN, counts)
    return counts.astype(jnp.int32)


def rising_rows(key, shape, fan_in, ratio):
    base = jax.random.truncated_normal(key, -4.0, 4.0, shape, jnp.float32)
    rows = jnp.arange(shape[1], dtype=jnp.float32) / (shape[1] - 1.0)
    log_ratio = jnp.log(jnp.float32(ratio))
    spread = jnp.sqrt((ratio * ratio - 1.0) / (2.0 * log_ratio))
    gain = jnp.exp(log_ratio * rows) / spread
    gain = gain.reshape((1, shape[1]) + (1,) * (len(shape) - 2))
    return base * gain * float(fan_in) ** (-0.5)


def draw_qkv_weight(key, part):
    key = jax.random.fold_in(key, 31)
    ratio = 3.0
    return rising_rows(key, (2, D, 3, D), D, ratio)


def draw_out_weight(key, part):
    key = jax.random.fold_in(key, 37)
    ratio = 3.0
    return rising_rows(key, (2, D, D), D // 16, ratio)


def draw_up_weight(key, part):
    key = jax.random.fold_in(key, 41)
    ratio = 3.0
    return rising_rows(key, (2, D, FF // D, D), D, ratio)


def draw_down_weight(key, part):
    key = jax.random.fold_in(key, 43)
    ratio = 3.0
    return rising_rows(key, (2, D, FF // D, D), FF, ratio)


def draw_ada_weight(key, part):
    key = jax.random.fold_in(key, 47)
    ratio = 3.0
    return rising_rows(key, (2, D, 6, D), D, ratio)


def block_scale(stream_key, extent, cuts, least, top_value):
    level, own = 1.0, jax.random.fold_in(stream_key, 6)
    for axis_at, shards_of in cuts:
        steps = jnp.exp(jax.random.uniform(jax.random.fold_in(own, axis_at), (shards_of,), jnp.float32, least / len(cuts), top_value / len(cuts)))
        level = level * jnp.repeat(steps, extent[axis_at] // shards_of).reshape([-1 if axis == axis_at else 1 for axis in range(len(extent))])
    return level


def noise(key, shape, scale, limit, cuts=(), kind=jnp.bfloat16):
    drawn = jax.random.normal(key, shape, jnp.float32) * scale
    if len(cuts) > 0:
        drawn = block_scale(key, shape, cuts, -0.22, 0.18) * drawn
    return jnp.clip(drawn, min=-limit, max=limit).astype(kind)


def setup_inputs(seed: int = 0) -> dict:
    streams_of = jax.random.split(jax.random.key(seed), 23)
    block_input = noise(streams_of[0], (TOKENS, D), 1.0, 6.0, ((0, 8), (1, 4)), jnp.float32)
    condition = noise(streams_of[1], (CLIPS, D), 1.0, 6.0, (), jnp.float32)
    frame_counts = draw_frame_counts(jax.random.fold_in(streams_of[22], 71), 0)
    cotangent = noise(streams_of[3], (TOKENS, D), 1.0, 6.0, ((0, 8), (1, 4)), jnp.float32)
    qkv_weight = draw_qkv_weight(jax.random.fold_in(streams_of[22], 71), 0)
    qkv_first = noise(streams_of[5], (2, D, 3, D), (0.1 * PARAMS ** -0.5), 0.00021362305, ((1, 8), (3, 4)), jnp.float32)
    qkv_second = jnp.clip(jnp.exp(math.log(8.36680030813497e-11) - 1.3862944 * jax.random.uniform(streams_of[6], (2, D, 3, D), jnp.float32) ** block_scale(streams_of[6], (2, D, 3, D), ((1, 8), (3, 4)), -0.2, 0.2)), 2.0917000770337424e-11, 8.36680030813497e-11)
    out_weight = draw_out_weight(jax.random.fold_in(streams_of[22], 71), 0)
    out_first = noise(streams_of[8], (2, D, D), (0.1 * PARAMS ** -0.5), 0.00021362305, ((1, 8), (2, 4)), jnp.float32)
    out_second = jnp.clip(jnp.exp(math.log(8.36680030813497e-11) - 1.3862944 * jax.random.uniform(streams_of[9], (2, D, D), jnp.float32) ** block_scale(streams_of[9], (2, D, D), ((1, 8), (2, 4)), -0.2, 0.2)), 2.0917000770337424e-11, 8.36680030813497e-11)
    up_weight = draw_up_weight(jax.random.fold_in(streams_of[22], 71), 0)
    up_first = noise(streams_of[11], (2, D, FF // D, D), (0.1 * PARAMS ** -0.5), 0.00021362305, ((1, 8), (3, 4)), jnp.float32)
    up_second = jnp.clip(jnp.exp(math.log(8.36680030813497e-11) - 1.3862944 * jax.random.uniform(streams_of[12], (2, D, FF // D, D), jnp.float32) ** block_scale(streams_of[12], (2, D, FF // D, D), ((1, 8), (3, 4)), -0.2, 0.2)), 2.0917000770337424e-11, 8.36680030813497e-11)
    down_weight = draw_down_weight(jax.random.fold_in(streams_of[22], 71), 0)
    down_first = noise(streams_of[14], (2, D, FF // D, D), (0.1 * PARAMS ** -0.5), 0.00021362305, ((1, 8), (3, 4)), jnp.float32)
    down_second = jnp.clip(jnp.exp(math.log(8.36680030813497e-11) - 1.3862944 * jax.random.uniform(streams_of[15], (2, D, FF // D, D), jnp.float32) ** block_scale(streams_of[15], (2, D, FF // D, D), ((1, 8), (3, 4)), -0.2, 0.2)), 2.0917000770337424e-11, 8.36680030813497e-11)
    ada_weight = draw_ada_weight(jax.random.fold_in(streams_of[22], 71), 0)
    ada_first = noise(streams_of[17], (2, D, 6, D), (0.1 * PARAMS ** -0.5), 0.00021362305, ((1, 8), (3, 4)), jnp.float32)
    ada_second = jnp.clip(jnp.exp(math.log(8.36680030813497e-11) - 1.3862944 * jax.random.uniform(streams_of[18], (2, D, 6, D), jnp.float32) ** block_scale(streams_of[18], (2, D, 6, D), ((1, 8), (3, 4)), -0.2, 0.2)), 2.0917000770337424e-11, 8.36680030813497e-11)
    bias_weight = noise(streams_of[19], (2, BIAS_ROWS, D), 0.3, 4.0, ((2, 4),), jnp.float32)
    bias_first = noise(streams_of[20], (2, BIAS_ROWS, D), (0.3 * PARAMS ** -0.5), 0.00061035156, ((2, 4),), jnp.float32)
    bias_second = jnp.clip(jnp.exp(math.log(8.366800585690726e-10) - 1.3862944 * jax.random.uniform(streams_of[21], (2, BIAS_ROWS, D), jnp.float32) ** block_scale(streams_of[21], (2, BIAS_ROWS, D), ((2, 4),), -0.2, 0.2)), 2.0917001464226814e-10, 8.366800585690726e-10)
    return dict(block_input=block_input, condition=condition, frame_counts=frame_counts, cotangent=cotangent, qkv_weight=qkv_weight, qkv_first=qkv_first, qkv_second=qkv_second, out_weight=out_weight, out_first=out_first, out_second=out_second, up_weight=up_weight, up_first=up_first, up_second=up_second, down_weight=down_weight, down_first=down_first, down_second=down_second, ada_weight=ada_weight, ada_first=ada_first, ada_second=ada_second, bias_weight=bias_weight, bias_first=bias_first, bias_second=bias_second)


HIGHEST_PREC = lax.Precision.HIGHEST
NORM_EPS = 1e-06
BETA_ONE = 0.9
BETA_TWO = 0.999
ADAM_EPS = 1e-06
WEIGHT_DECAY = 0.01
LEARN_RATE = 0.5
CLIP_LIMIT = 1.0
MASKED = -1e+30

@jax.custom_vjp
def low(v):
    return lax.optimization_barrier(v.astype(jnp.bfloat16)).astype(jnp.float32)

@jax.custom_vjp
def low_back(v):
    return v

def low_keep(v):
    return (low(v), None)

def low_pass(kept, grad):
    return (grad,)

def back_keep(v):
    return (v, None)

def back_low(kept, grad):
    return (low(grad),)
low.defvjp(low_keep, low_pass)
low_back.defvjp(back_keep, back_low)

def low_both(value_in):
    return low(low_back(value_in))

def normalize(rows_in):
    row_mean = lax.optimization_barrier(jnp.mean(rows_in, axis=-1, keepdims=True))
    centered = rows_in - row_mean
    return centered * lax.rsqrt(lax.optimization_barrier(jnp.mean(centered * centered, axis=-1, keepdims=True)) + NORM_EPS)

def attend(queries, key_rows, value_rows, key_mask):
    scores = low_back(jnp.einsum('blhe,bmhe->bhlm', queries, key_rows, precision=HIGHEST_PREC) * HEAD_DIM ** (-0.5))
    scores = jnp.where(key_mask[:, None, None, :], scores, MASKED)
    attn_probs = low(jax.nn.softmax(scores, axis=-1))
    return low_both(jnp.einsum('bhlm,bmhe->blhe', attn_probs, value_rows, precision=HIGHEST_PREC))

def layer_forward(residual, modul, params, temporal, valid):
    w_qkv, w_out, w_up, w_down, bias_rows = params
    expand = FF // D
    rows_all = residual.shape[0]
    hidden_one = low(normalize(low(residual)) * (1.0 + modul[1]) + modul[0])
    zero_row = jnp.zeros_like(bias_rows[0])
    qkv_rows = jnp.einsum('rd,dke->rke', hidden_one, low(w_qkv), precision=HIGHEST_PREC) + jnp.stack([bias_rows[0], zero_row, bias_rows[1]])
    queries = low_both(qkv_rows[:, 0]).reshape(CLIP_LEN, PATCHES, HEADS, HEAD_DIM)
    key_rows = low_both(qkv_rows[:, 1]).reshape(CLIP_LEN, PATCHES, HEADS, HEAD_DIM)
    value_rows = low_both(qkv_rows[:, 2]).reshape(CLIP_LEN, PATCHES, HEADS, HEAD_DIM)
    if temporal:
        key_mask = jnp.broadcast_to(valid[None, :], (PATCHES, CLIP_LEN))
        heads_out = attend(jnp.transpose(queries, (1, 0, 2, 3)), jnp.transpose(key_rows, (1, 0, 2, 3)), jnp.transpose(value_rows, (1, 0, 2, 3)), key_mask)
        heads_out = jnp.transpose(heads_out, (1, 0, 2, 3))
    else:
        key_mask = jnp.ones((CLIP_LEN, PATCHES), dtype=bool)
        heads_out = attend(queries, key_rows, value_rows, key_mask)
    heads_out = heads_out.reshape(rows_all, D)
    attn_branch = low_back(jnp.einsum('re,de->rd', heads_out, low(w_out), precision=HIGHEST_PREC) + bias_rows[2])
    middle = residual + modul[2] * attn_branch
    hidden_two = low(normalize(low(middle)) * (1.0 + modul[4]) + modul[3])
    upper = low_back(jnp.einsum('rd,dke->rke', hidden_two, low(w_up), precision=HIGHEST_PREC) + bias_rows[3:3 + expand])
    active = low(jax.nn.gelu(upper, approximate=True))
    mlp_branch = low_back(jnp.einsum('rke,dke->rd', active, low(w_down), precision=HIGHEST_PREC) + bias_rows[3 + expand])
    return middle + modul[5] * mlp_branch

def clip_forward(rows_in, params, silu_cond, valid):
    qkv_w, out_w, up_w, down_w, ada_w, bias_w = params
    expand = FF // D
    residual = rows_in
    for layer_idx in range(2):
        modul = jnp.einsum('d,dke->ke', silu_cond, ada_w[layer_idx], precision=HIGHEST_PREC) + bias_w[layer_idx, 4 + expand:10 + expand]
        residual = layer_forward(residual, modul, (qkv_w[layer_idx], out_w[layer_idx], up_w[layer_idx], down_w[layer_idx], bias_w[layer_idx]), layer_idx == 1, valid)
    return residual

def reference(block_input, condition, frame_counts, cotangent, qkv_weight, qkv_first, qkv_second, out_weight, out_first, out_second, up_weight, up_first, up_second, down_weight, down_first, down_second, ada_weight, ada_first, ada_second, bias_weight, bias_first, bias_second):
    params = (qkv_weight, out_weight, up_weight, down_weight, ada_weight, bias_weight)
    clip_rows = CLIP_LEN * PATCHES
    inputs = block_input.reshape(CLIPS, clip_rows, D)
    cotangents = cotangent.reshape(CLIPS, clip_rows, D)

    def one_clip(summed, item):
        rows_in, cond_row, frame_count, cot_rows = item
        silu_cond = jax.nn.silu(cond_row)
        valid = jnp.arange(CLIP_LEN, dtype=jnp.int32) < frame_count
        outputs, pullback = jax.vjp(lambda rows_val, param_val: clip_forward(rows_val, param_val, silu_cond, valid), rows_in, params)
        grad_rows, grad_params = pullback(cot_rows)
        return (jax.tree.map(jnp.add, summed, grad_params), (outputs, grad_rows))
    zeros = jax.tree.map(jnp.zeros_like, params)
    gradients, (outputs, grad_rows) = lax.scan(one_clip, zeros, (inputs, condition, frame_counts, cotangents))
    total_sq = jnp.zeros((), jnp.float32)
    for gradient in gradients:
        total_sq = total_sq + jnp.sum(gradient * gradient)
    grad_norm = jnp.sqrt(total_sq)
    factor = jnp.minimum(1.0, CLIP_LIMIT / grad_norm)
    first_fix = 1.0 - BETA_ONE ** STEP
    second_fix = 1.0 - BETA_TWO ** STEP
    firsts = (qkv_first, out_first, up_first, down_first, ada_first, bias_first)
    seconds = (qkv_second, out_second, up_second, down_second, ada_second, bias_second)
    results = []
    norm_terms = []
    for master, first_in, second_in, gradient in zip(params, firsts, seconds, gradients):
        clipped = gradient * factor
        moment = BETA_ONE * first_in + (1.0 - BETA_ONE) * clipped
        square = BETA_TWO * second_in + (1.0 - BETA_TWO) * clipped * clipped
        update = moment / first_fix / (jnp.sqrt(square / second_fix) + ADAM_EPS) + WEIGHT_DECAY * master
        weight_norm = jnp.sqrt(lax.optimization_barrier(jnp.sum((master * master).reshape(2, -1), axis=1)))
        update_norm = jnp.sqrt(lax.optimization_barrier(jnp.sum((update * update).reshape(2, -1), axis=1)))
        trust_ratio = (weight_norm / update_norm).reshape((2,) + (1,) * (master.ndim - 1))
        results.append((master - LEARN_RATE * trust_ratio * update, moment, square))
        norm_terms.append(jnp.stack([weight_norm, update_norm], axis=1))
    trust_norms = jnp.stack(norm_terms, axis=1)
    return (outputs.reshape(TOKENS, D), grad_rows.reshape(TOKENS, D), results[0][0], results[0][1], results[0][2], results[1][0], results[1][1], results[1][2], results[2][0], results[2][1], results[2][2], results[3][0], results[3][1], results[3][2], results[4][0], results[4][1], results[4][2], results[5][0], results[5][1], results[5][2], trust_norms, grad_norm.reshape(1))
```

```python
import functools

import jax
import jax.numpy as jnp
from jax import lax
from jax.experimental import pallas as pl
from jax.experimental.pallas import tpu as pltpu
from jax.sharding import PartitionSpec as P

HEAD_DIM = 72
PATCHES = 256
CLIP_LEN = 16
STEP = 10
KINDS = 12


HIGHEST_PREC = lax.Precision.HIGHEST
NORM_EPS = 1e-06
BETA_ONE = 0.9
BETA_TWO = 0.999
ADAM_EPS = 1e-06
WEIGHT_DECAY = 0.01
LEARN_RATE = 0.5
CLIP_LIMIT = 1.0
MASKED = -1e30
MESH = pl.DeviceIdType.MESH
BF16 = jnp.bfloat16
F32 = jnp.float32


def greet(partners):
    barrier = pltpu.get_barrier_semaphore()
    count = 0
    for wide_to, narrow_to, cond in partners:

        def send(wide_to=wide_to, narrow_to=narrow_to):
            pl.semaphore_signal(
                barrier, inc=1, device_id=(wide_to, narrow_to), device_id_type=MESH
            )

        if cond is None:
            send()
            count = count + 1
        else:
            pl.when(cond)(send)
            count = count + jnp.where(cond, 1, 0)
    pl.semaphore_wait(barrier, count)


def begin_swaps(groups, narrow_count, sources, targets, local_sem, send_sem, recv_sem, others=()):
    total = len(groups)
    wide_at, narrow_at = lax.axis_index("wide"), lax.axis_index("narrow")
    half = wide_at % 2

    def member(size, index):
        if size == narrow_count:
            return wide_at, index
        return wide_at - half + index // narrow_count, index % narrow_count

    largest = max(groups)
    me_of = {narrow_count: narrow_at, 2 * narrow_count: half * narrow_count + narrow_at}

    def keep(at):
        me = me_of[groups[at]]
        return pltpu.make_async_copy(sources[at].at[me], targets[at].at[me], local_sem.at[at])

    def exchange(at, step, out_at, in_at, to):
        return pltpu.make_async_remote_copy(
            src_ref=sources[at].at[out_at],
            dst_ref=targets[at].at[in_at],
            send_sem=send_sem.at[at, step],
            recv_sem=recv_sem.at[at, step],
            device_id=member(groups[at], to),
            device_id_type=MESH,
        )

    def each():
        for step in range(1, largest):
            for at in range(total):
                if step < groups[at]:
                    yield at, step, groups[at], me_of[groups[at]]

    for at in range(total):
        keep(at).start()
    greet(
        [
            member(largest, (me_of[largest] + step) % largest) + (None,)
            for step in range(1, largest)
        ]
        + list(others)
    )
    for at, step, size, me in each():
        there = (me + step) % size
        exchange(at, step, there, me, there).start()

    def finish():
        for at in range(total):
            keep(at).wait()
        for at, step, size, me in each():
            there = (me + step) % size
            exchange(at, step, there, me, there).wait_send()
            origin = (me + size - step) % size
            exchange(at, step, origin, origin, origin).wait_recv()

    return finish


def swap_kernel(groups, narrow_count, *refs):
    total = len(groups)
    begin_swaps(groups, narrow_count, refs[:total], refs[total : 2 * total], *refs[2 * total :])()


def swap(arrays, collective_id, name):
    narrow_count = lax.axis_size("narrow")
    groups = tuple(a.shape[0] for a in arrays)
    total = len(arrays)
    largest = max(groups)
    return pl.pallas_call(
        functools.partial(swap_kernel, groups, narrow_count),
        out_shape=[jax.ShapeDtypeStruct(a.shape, a.dtype) for a in arrays],
        in_specs=[pl.BlockSpec(memory_space=pl.ANY)] * total,
        out_specs=[pl.BlockSpec(memory_space=pl.ANY)] * total,
        scratch_shapes=[
            pltpu.SemaphoreType.DMA((total,)),
            pltpu.SemaphoreType.DMA((total, largest)),
            pltpu.SemaphoreType.DMA((total, largest)),
        ],
        compiler_params=pltpu.CompilerParams(
            collective_id=collective_id, has_side_effects=True
        ),
        name=name,
    )(*arrays)


def places():
    wide_at, narrow_at = lax.axis_index("wide"), lax.axis_index("narrow")
    x_at, z_at = wide_at % 2, wide_at // 2
    core, y_at = narrow_at % 2, narrow_at // 2
    flip_x, flip_y = 1 - 2 * x_at, 2 - 4 * y_at
    first = (wide_at + (1 - core) * flip_x, narrow_at + core * flip_y)
    second = (wide_at + core * flip_x, narrow_at + (1 - core) * flip_y)
    sibling = (wide_at, narrow_at + 1 - 2 * core)
    return wide_at, narrow_at, x_at, z_at, first, second, sibling


def gather_kernel(layers, lines, own_ref, *refs):
    fulls = refs[:layers]
    local_sem, zs_sem, zr_sem, ps_sem, pr_sem = refs[layers:]
    wide_at, narrow_at, x_at, z_at, first, second, sibling = places()
    chunks = [(layer, j) for layer in range(layers) for j in range(3)]

    def own_block(q):
        layer, j = chunks[q]
        return pltpu.make_async_copy(
            own_ref.at[layer, j],
            fulls[layer].at[3 * narrow_at + j, z_at, x_at],
            local_sem.at[q],
        )

    for q in range(len(chunks)):
        own_block(q).start()
    up_ok, down_ok = z_at + 1 < lines, z_at >= 1
    greet(
        [
            (wide_at + 2, narrow_at, up_ok),
            (wide_at - 2, narrow_at, down_ok),
            first + (None,),
            second + (None,),
            sibling + (None,),
        ]
    )

    def hop(q, up, h, origin):
        layer, j = chunks[q]
        block = fulls[layer].at[3 * narrow_at + j, origin, x_at]
        return pltpu.make_async_remote_copy(
            src_ref=block,
            dst_ref=block,
            send_sem=zs_sem.at[q, up, h],
            recv_sem=zr_sem.at[q, up, h],
            device_id=(wide_at + (2 if up else -2), narrow_at),
            device_id_type=MESH,
        )

    def hop_sends(q, h, act):
        pl.when(jnp.logical_and(up_ok, z_at - h >= 0))(
            lambda: act(hop(q, 1, h, z_at - h))
        )
        pl.when(jnp.logical_and(down_ok, z_at + h < lines))(
            lambda: act(hop(q, 0, h, z_at + h))
        )

    def hop_receives(q, h):
        pl.when(z_at - 1 - h >= 0)(lambda: hop(q, 1, h, z_at - 1 - h).wait_recv())
        pl.when(z_at + 1 + h < lines)(lambda: hop(q, 0, h, z_at + 1 + h).wait_recv())

    def plane(q, slot, narrow_of, x_of, partner):
        layer, j = chunks[q]
        column = fulls[layer].at[3 * narrow_of + j, :, x_of]
        return pltpu.make_async_remote_copy(
            src_ref=column,
            dst_ref=column,
            send_sem=ps_sem.at[q, slot],
            recv_sem=pr_sem.at[q, slot],
            device_id=partner,
            device_id_type=MESH,
        )

    me = (narrow_at, x_at)
    one = (first[1], first[0] % 2)
    two = (second[1], second[0] % 2)
    both = (first[1] + second[1] - narrow_at, 1 - x_at)
    sends = [
        (me, first),
        (me, second),
        (one, second),
        (me, sibling),
        (one, sibling),
        (two, sibling),
        (both, sibling),
    ]
    over = sibling[1] - narrow_at
    arrivals = [
        one,
        two,
        both,
        (me[0] + over, me[1]),
        (one[0] + over, one[1]),
        (two[0] + over, two[1]),
        (both[0] + over, both[1]),
    ]

    def send(q, slot):
        plane(q, slot, *sends[slot][0], sends[slot][1]).start()

    def receive(q, slot):
        plane(q, slot, *arrivals[slot], sends[slot][1]).wait_recv()

    stages = lines + 3

    def stage(q, s):
        if s == 0:
            own_block(q).wait()
            if lines > 1:
                hop_sends(q, 0, lambda copy: copy.start())
        elif s < lines - 1:
            hop_receives(q, s - 1)
            hop_sends(q, s, lambda copy: copy.start())
        elif s == lines - 1:
            hop_receives(q, s - 1)
        if s == lines - 1:
            send(q, 0)
            send(q, 1)
            send(q, 3)
        if s == lines:
            receive(q, 0)
            send(q, 2)
            send(q, 4)
        if s == lines + 1:
            receive(q, 1)
            send(q, 5)
            receive(q, 2)
            send(q, 6)
        if s == lines + 2:
            for slot in range(3, 7):
                receive(q, slot)

    for t in range(len(chunks) + stages - 1):
        for q in range(len(chunks)):
            if 0 <= t - q < stages:
                stage(q, t - q)
    for q in range(len(chunks)):
        for h in range(lines - 1):
            hop_sends(q, h, lambda copy: copy.wait_send())
        for slot in range(7):
            plane(q, slot, *sends[slot][0], sends[slot][1]).wait_send()


def gather_weights(own, collective_id):
    layers, per, rows, width = own.shape
    wide_count = lax.axis_size("wide")
    lines = wide_count // 2
    chunks = layers * per
    fulls = pl.pallas_call(
        functools.partial(gather_kernel, layers, lines),
        out_shape=[
            jax.ShapeDtypeStruct((KINDS, lines, 2, rows, width), own.dtype)
            for _ in range(layers)
        ],
        in_specs=[pl.BlockSpec(memory_space=pl.ANY)],
        out_specs=[pl.BlockSpec(memory_space=pl.ANY)] * layers,
        scratch_shapes=[
            pltpu.SemaphoreType.DMA((chunks,)),
            pltpu.SemaphoreType.DMA((chunks, 2, max(lines - 1, 1))),
            pltpu.SemaphoreType.DMA((chunks, 2, max(lines - 1, 1))),
            pltpu.SemaphoreType.DMA((chunks, 7)),
            pltpu.SemaphoreType.DMA((chunks, 7)),
        ],
        compiler_params=pltpu.CompilerParams(
            collective_id=collective_id, has_side_effects=True
        ),
        cost_estimate=pl.CostEstimate(
            flops=0, bytes_accessed=900_000_000, transcendentals=0
        ),
        name="gather_weights",
    )(own)
    return [full.reshape(KINDS, wide_count * rows, width) for full in fulls]


def scatter_kernel(lines, rows, swaps, swap_groups, narrow_count, *refs):
    layers = 2
    chunks = 3 * layers
    acts = [refs[8 * layer : 8 * layer + 8] for layer in range(layers)]
    at = 8 * layers
    swap_from = refs[at : at + swaps]
    out_ref = refs[at + swaps]
    swap_to = refs[at + swaps + 1 : at + 2 * swaps + 1]
    (
        in_a,
        in_b,
        grads,
        from_core,
        from_second,
        from_first,
        from_line,
        pieces,
        in_sem,
        s1,
        r1,
        s2,
        r2,
        s3,
        r3,
        zs,
        zr,
        fs,
        fr,
        swap_local,
        swap_send,
        swap_recv,
        free_core,
        free_second,
        free_first,
        free_line,
    ) = refs[at + 2 * swaps + 1 :]
    wide_at, narrow_at, x_at, z_at, first, second, sibling = places()
    core = narrow_at % 2
    width = grads.shape[-1]
    col_width = width // narrow_count
    up_ok, down_ok = z_at + 1 < lines, z_at >= 1
    z_mirror = lines - 1 - z_at

    def operands(q, owner):
        hidden_one, grad_qkv, grad_attn, heads, hidden_two, grad_upper, grad_mlp, active = acts[
            q // 3
        ]
        kind = 3 * owner + q % 3
        if kind < 3:
            return hidden_one, grad_qkv.at[kind]
        if kind == 3:
            return grad_attn, heads
        if kind < 8:
            return hidden_two, grad_upper.at[kind - 4]
        return grad_mlp, active.at[kind - 8]

    def load(q, owner):
        for i in range(chunks):

            def start(i=i):
                left, right = operands(i, owner)
                pltpu.make_async_copy(
                    left, in_a.at[owner % 2], in_sem.at[owner % 2, 0]
                ).start()
                pltpu.make_async_copy(
                    right, in_b.at[owner % 2], in_sem.at[owner % 2, 1]
                ).start()

            pl.when(q == i)(start)

    def loaded(owner):
        left, right = operands(0, owner)
        pltpu.make_async_copy(left, in_a.at[owner % 2], in_sem.at[owner % 2, 0]).wait()
        pltpu.make_async_copy(right, in_b.at[owner % 2], in_sem.at[owner % 2, 1]).wait()

    load(0, 0)
    finish_swaps = begin_swaps(
        swap_groups,
        narrow_count,
        swap_from,
        swap_to,
        swap_local,
        swap_send,
        swap_recv,
        [(wide_at + 2, narrow_at, up_ok), (wide_at - 2, narrow_at, down_ok)],
    )

    def to_core(slot, owner):
        return pltpu.make_async_remote_copy(
            src_ref=grads.at[slot, owner],
            dst_ref=from_core.at[slot, owner // 2],
            send_sem=s1.at[slot, owner // 2],
            recv_sem=r1.at[slot, owner // 2],
            device_id=sibling,
            device_id_type=MESH,
        )

    two = (second[1], second[0] % 2)
    both = (first[1] + second[1] - narrow_at, 1 - x_at)
    one = (first[1], first[0] % 2)

    def to_second(slot, place):
        owner, x_of = (two, both)[place]
        return pltpu.make_async_remote_copy(
            src_ref=grads.at[slot, owner, :, x_of],
            dst_ref=from_second.at[slot, place],
            send_sem=s2.at[slot, place],
            recv_sem=r2.at[slot, place],
            device_id=second,
            device_id_type=MESH,
        )

    def to_first(slot):
        return pltpu.make_async_remote_copy(
            src_ref=from_second.at[slot, 1],
            dst_ref=from_first.at[slot],
            send_sem=s3.at[slot],
            recv_sem=r3.at[slot],
            device_id=first,
            device_id_type=MESH,
        )

    def target(up, s):
        return lines - 1 - s + z_at if up else s - z_mirror

    def to_line(slot, up, s, place):
        return pltpu.make_async_remote_copy(
            src_ref=from_first.at[slot, place],
            dst_ref=from_line.at[slot, up, s],
            send_sem=zs.at[slot, up, s],
            recv_sem=zr.at[slot, up, s],
            device_id=(wide_at + (2 if up else -2), narrow_at),
            device_id_type=MESH,
        )

    def to_owner(q, slot, step):
        there = (narrow_at + step) % narrow_count
        return pltpu.make_async_remote_copy(
            src_ref=pieces.at[slot, there],
            dst_ref=out_ref.at[1 - q // 3, 3 * narrow_at + q % 3],
            send_sem=fs.at[slot, step],
            recv_sem=fr.at[q, step],
            device_id=(wide_at, there),
            device_id_type=MESH,
        )

    def keep_own(q, slot):
        return pltpu.make_async_copy(
            pieces.at[slot, narrow_at],
            out_ref.at[1 - q // 3, 3 * narrow_at + q % 3],
            fs.at[slot, 0],
        )

    def compute(q):
        slot = q % 2
        pl.when(q >= 2)(lambda: pl.semaphore_wait(free_core, 1))
        for owner in range(4):
            if owner < 3:
                load(q, owner + 1)
            else:
                load(q + 1, 0)
            loaded(owner)
            place = owner % 2
            tile = 384 if width % 384 == 0 else width

            def columns(i, carry, owner=owner, place=place, tile=tile):
                cols = pl.ds(pl.multiple_of(i * tile, 128), tile)
                total = lax.dot_general(
                    in_a[place],
                    in_b[place, :, cols],
                    (((0,), (0,)), ((), ())),
                    preferred_element_type=F32,
                ).astype(BF16)
                for z in range(lines):
                    for x in range(2):
                        start = (2 * z + x) * rows
                        grads[slot, owner, z, x, :, cols] = total[start : start + rows]
                return carry

            lax.fori_loop(0, width // tile, columns, 0)
            pl.when(core != owner % 2)(lambda owner=owner: to_core(slot, owner).start())

    def add_core(q):
        slot = q % 2
        for half in range(2):
            to_core(slot, 2 * half).wait_recv()
            mine = 2 * half + core

            def body(z, carry, half=half, mine=mine):
                for x in range(2):
                    grads[slot, mine, z, x] = grads[slot, mine, z, x] + from_core[slot, half, z, x]
                return carry

            lax.fori_loop(0, lines, body, 0)
        for half in range(2):
            to_core(slot, 2 * half + 1).wait_send()
        pl.when(q + 2 < chunks)(
            lambda: pl.semaphore_signal(
                free_core, inc=1, device_id=sibling, device_id_type=MESH
            )
        )
        pl.when(q >= 2)(lambda: pl.semaphore_wait(free_second, 1))
        to_second(slot, 1).start()
        to_second(slot, 0).start()

    def add_second(q):
        slot = q % 2
        for place in (1, 0):
            owner, x_of = ((narrow_at, x_at), one)[place]
            to_second(slot, place).wait_recv()

            def body(z, carry, place=place, owner=owner, x_of=x_of):
                from_second[slot, place, z] = (
                    from_second[slot, place, z] + grads[slot, owner, z, x_of]
                )
                return carry

            lax.fori_loop(0, lines, body, 0)
            if place == 1:
                pl.when(q >= 2)(lambda: pl.semaphore_wait(free_first, 1))
                to_first(slot).start()
        for place in (1, 0):
            to_second(slot, place).wait_send()

    def line_hop(q, s):
        slot = q % 2
        for up in (1, 0):
            here = z_at if up else z_mirror
            place = target(up, s)
            if s >= 1:

                def take(up=up, place=place):
                    to_line(slot, up, s - 1, 0).wait_recv()
                    from_first[slot, place] = from_first[slot, place] + from_line[slot, up, s - 1]

                pl.when(jnp.logical_and(here >= 1, here <= s))(take)
            if s < lines - 1:
                pl.when(here <= s)(
                    lambda up=up, place=place: to_line(slot, up, s, place).start()
                )

    def add_first(q):
        slot = q % 2
        to_first(slot).wait_recv()

        def body(z, carry):
            from_first[slot, z] = from_first[slot, z] + from_second[slot, 0, z]
            return carry

        lax.fori_loop(0, lines, body, 0)
        to_first(slot).wait_send()
        pl.when(q + 2 < chunks)(
            lambda: pl.semaphore_signal(
                free_second, inc=1, device_id=second, device_id_type=MESH
            )
        )
        if lines > 1:
            pl.when(jnp.logical_and(q >= 2, up_ok))(
                lambda: pl.semaphore_wait(free_line.at[1], 1)
            )
            pl.when(jnp.logical_and(q >= 2, down_ok))(
                lambda: pl.semaphore_wait(free_line.at[0], 1)
            )
            line_hop(q, 0)

    def finish(q):
        slot = q % 2
        if lines > 1:
            line_hop(q, lines - 1)
            for s in range(lines - 1):
                pl.when(z_at <= s)(lambda s=s: to_line(slot, 1, s, 0).wait_send())
                pl.when(z_mirror <= s)(lambda s=s: to_line(slot, 0, s, 0).wait_send())
            pl.when(jnp.logical_and(q + 2 < chunks, down_ok))(
                lambda: pl.semaphore_signal(
                    free_line.at[1],
                    inc=1,
                    device_id=(wide_at - 2, narrow_at),
                    device_id_type=MESH,
                )
            )
            pl.when(jnp.logical_and(q + 2 < chunks, up_ok))(
                lambda: pl.semaphore_signal(
                    free_line.at[0],
                    inc=1,
                    device_id=(wide_at + 2, narrow_at),
                    device_id_type=MESH,
                )
            )

        def release(last):
            keep_own(last, last % 2).wait()
            for step in range(1, narrow_count):
                to_owner(last, last % 2, step).wait_send()

        pl.when(q >= 2)(lambda: release(q - 2))
        total = from_first[slot, z_at]
        for there in range(narrow_count):
            pieces[slot, there] = total[:, there * col_width : (there + 1) * col_width]
        pl.when(q + 2 < chunks)(
            lambda: pl.semaphore_signal(
                free_first, inc=1, device_id=first, device_id_type=MESH
            )
        )
        keep_own(q, slot).start()
        for step in range(1, narrow_count):
            to_owner(q, slot, step).start()
        return release

    def iteration(t, carry):
        def when(lag, act):
            q = t - lag
            pl.when(jnp.logical_and(q >= 0, q < chunks))(lambda: act(q))

        when(3, add_first)
        when(1, add_core)
        if lines > 2:
            when(3, lambda q: line_hop(q, 1))
        when(2, add_second)

        def rest(q):
            for s in range(2, lines - 1):
                line_hop(q, s)

        if lines > 3:
            when(3, rest)
        when(0, compute)
        when(3, lambda q: finish(q) and None)
        return carry

    lax.fori_loop(0, chunks + 3, iteration, 0)
    for last in (chunks - 2, chunks - 1):
        keep_own(last, last % 2).wait()
        for step in range(1, narrow_count):
            to_owner(last, last % 2, step).wait_send()

    def arrived(q, carry):
        for step in range(1, narrow_count):
            to_owner(q, 0, step).wait_recv()
        return carry

    lax.fori_loop(0, chunks, arrived, 0)
    finish_swaps()


def scatter_grads(acts, moves, rows, collective_id):
    wide_count, narrow_count = lax.axis_size("wide"), lax.axis_size("narrow")
    lines = wide_count // 2
    tokens, width = acts[0].shape
    col_width = width // narrow_count
    chunks = 6
    swaps = len(moves)
    groups = tuple(a.shape[0] for a in moves)
    largest = max(groups)
    dma = pltpu.SemaphoreType.DMA
    regular = pltpu.SemaphoreType.REGULAR
    block = (lines, 2, rows, width)
    any_spec = pl.BlockSpec(memory_space=pl.ANY)
    results = pl.pallas_call(
        functools.partial(scatter_kernel, lines, rows, swaps, groups, narrow_count),
        out_shape=[jax.ShapeDtypeStruct((2, KINDS, rows, col_width), BF16)]
        + [jax.ShapeDtypeStruct(a.shape, a.dtype) for a in moves],
        in_specs=[any_spec] * (len(acts) + swaps),
        out_specs=[any_spec] * (1 + swaps),
        scratch_shapes=[
            pltpu.VMEM((2, tokens, width), BF16),
            pltpu.VMEM((2, tokens, width), BF16),
            pltpu.VMEM((2, 4) + block, BF16),
            pltpu.VMEM((2, 2) + block, BF16),
            pltpu.VMEM((2, 2, lines, rows, width), BF16),
            pltpu.VMEM((2, lines, rows, width), BF16),
            pltpu.VMEM((2, 2, max(lines - 1, 1), rows, width), BF16),
            pltpu.VMEM((2, narrow_count, rows, col_width), BF16),
            dma((2, 2)),
            dma((2, 2)),
            dma((2, 2)),
            dma((2, 2)),
            dma((2, 2)),
            dma((2,)),
            dma((2,)),
            dma((2, 2, max(lines - 1, 1))),
            dma((2, 2, max(lines - 1, 1))),
            dma((2, narrow_count)),
            dma((chunks, narrow_count)),
            dma((swaps,)),
            dma((swaps, largest)),
            dma((swaps, largest)),
            regular,
            regular,
            regular,
            regular((2,)),
        ],
        compiler_params=pltpu.CompilerParams(
            collective_id=collective_id,
            has_side_effects=True,
            vmem_limit_bytes=61 * 1024 * 1024,
        ),
        cost_estimate=pl.CostEstimate(
            flops=2 * 2 * KINDS * width * width * tokens,
            bytes_accessed=900_000_000,
            transcendentals=0,
        ),
        name="scatter_grads",
    )(*acts, *moves)
    return results[0], results[1:]


def normalize(full_rows):
    row_mean = jnp.mean(full_rows, axis=-1, keepdims=True)
    centered = full_rows - row_mean
    inverse = lax.rsqrt(jnp.mean(centered * centered, axis=-1, keepdims=True) + NORM_EPS)
    return (centered * inverse, inverse)


def norm_modulate(residual, shift_vec, scale_vec):
    normed, inverse = normalize(residual.astype(BF16).astype(F32))
    hidden = (normed * (1.0 + scale_vec) + shift_vec).astype(BF16)
    return (normed, inverse, hidden)


def norm_backward(grad_hidden, normed, inverse, scale_vec):
    grad_normed = grad_hidden * (1.0 + scale_vec)
    row_first = jnp.mean(grad_normed, axis=-1, keepdims=True)
    row_second = jnp.mean(grad_normed * normed, axis=-1, keepdims=True)
    grad_input = inverse * (grad_normed - row_first - normed * row_second)
    return (grad_input, jnp.sum(grad_hidden, axis=0), jnp.sum(grad_hidden * normed, axis=0))


def masked_scores(queries, key_rows, key_mask):
    head_scale = queries.shape[-1] ** (-0.5)
    scores = (
        jnp.einsum("blhe,bmhe->bhlm", queries, key_rows, preferred_element_type=F32) * head_scale
    )
    if key_mask is not None:
        scores = jnp.where(key_mask[None, None], scores, MASKED)
    return (scores, head_scale)


def attend_forward(queries, key_rows, value_rows, key_mask):
    scores, _ = masked_scores(queries, key_rows, key_mask)
    row_max = jnp.max(scores, axis=-1, keepdims=True)
    raised = jnp.exp(scores - row_max)
    summed = jnp.sum(raised, axis=-1, keepdims=True)
    attn_probs = (raised / summed).astype(BF16)
    outputs = jnp.einsum("bhlm,bmhe->blhe", attn_probs, value_rows, preferred_element_type=F32)
    return (outputs.astype(BF16), (row_max, summed))


def attend_backward(queries, key_rows, value_rows, key_mask, softmax_stats, grad_outputs):
    row_max, summed = softmax_stats
    scores, head_scale = masked_scores(queries, key_rows, key_mask)
    attn_probs = jnp.exp(scores - row_max) / summed
    grad_probs = jnp.einsum(
        "blhe,bmhe->bhlm", grad_outputs, value_rows, preferred_element_type=F32
    )
    row_delta = jnp.sum(grad_probs * attn_probs, axis=-1, keepdims=True)
    grad_scores = (attn_probs * (grad_probs - row_delta)).astype(BF16)
    grad_queries = (
        jnp.einsum("bhlm,bmhe->blhe", grad_scores, key_rows, preferred_element_type=F32)
        * head_scale
    ).astype(BF16)
    grad_keys = (
        jnp.einsum("bhlm,blhe->bmhe", grad_scores, queries, preferred_element_type=F32)
        * head_scale
    ).astype(BF16)
    grad_values = jnp.einsum(
        "bhlm,blhe->bmhe", attn_probs.astype(BF16), grad_outputs, preferred_element_type=F32
    ).astype(BF16)
    return (grad_queries, grad_keys, grad_values)


def split_heads(rows, length):
    tokens, width = rows.shape
    return rows.reshape(tokens // length, length, width // HEAD_DIM, HEAD_DIM)


def forward_block(residual, modul, weights, bias_rows, length, key_mask):
    expand = (KINDS - 4)//2
    tokens, width = residual.shape
    normed_one, inverse_one, hidden_one = norm_modulate(residual, modul[0], modul[1])
    qkv_bias = jnp.stack([bias_rows[0], jnp.zeros_like(bias_rows[0]), bias_rows[1]])
    qkv_rows = (
        jnp.einsum("td,kde->kte", hidden_one, weights[0:3], preferred_element_type=F32)
        + qkv_bias[:, None, :]
    ).astype(BF16)
    arranged = [split_heads(qkv_rows[kind], length) for kind in range(3)]
    outputs, softmax_stats = attend_forward(*arranged, key_mask)
    heads_out = outputs.reshape(tokens, width)
    attn_branch = (
        jnp.einsum("te,de->td", heads_out, weights[3], preferred_element_type=F32) + bias_rows[2]
    )
    middle = residual + modul[2] * attn_branch
    normed_two, inverse_two, hidden_two = norm_modulate(middle, modul[3], modul[4])
    upper = (
        jnp.einsum("td,kde->kte", hidden_two, weights[4 : 4 + expand], preferred_element_type=F32)
        + bias_rows[3 : 3 + expand][:, None, :]
    )
    active = jax.nn.gelu(upper, approximate=True).astype(BF16)
    mlp_branch = (
        jnp.einsum("kte,kde->td", active, weights[4 + expand :], preferred_element_type=F32)
        + bias_rows[3 + expand]
    )
    output = middle + modul[5] * mlp_branch
    kept_vals = (
        normed_one,
        inverse_one,
        hidden_one,
        heads_out,
        (arranged, softmax_stats),
        attn_branch,
        normed_two,
        inverse_two,
        hidden_two,
        upper,
        active,
        mlp_branch,
    )
    return (output, kept_vals)


def backward_block(grad_out, kept_vals, modul, weights, length, key_mask):
    (
        normed_one,
        inverse_one,
        hidden_one,
        heads_out,
        kept_attn,
        attn_branch,
        normed_two,
        inverse_two,
        hidden_two,
        upper,
        active,
        mlp_branch,
    ) = kept_vals
    expand = (KINDS - 4)//2
    tokens, width = grad_out.shape
    arranged, softmax_stats = kept_attn
    grad_mlp = (grad_out * modul[5]).astype(BF16)
    grad_gate_two = jnp.sum(grad_out * mlp_branch, axis=0)
    grad_active = jnp.einsum(
        "td,kde->kte", grad_mlp, weights[4 + expand :], preferred_element_type=F32
    )
    gelu_pull = jax.vjp(lambda value_in: jax.nn.gelu(value_in, approximate=True), upper)[1]
    grad_upper = gelu_pull(grad_active)[0].astype(BF16)
    grad_hidden_two = jnp.einsum(
        "kte,kde->td", grad_upper, weights[4 : 4 + expand], preferred_element_type=F32
    )
    grad_norm_two, grad_shift_two, grad_scale_two = norm_backward(
        grad_hidden_two, normed_two, inverse_two, modul[4]
    )
    grad_middle = grad_out + grad_norm_two
    grad_attn = (grad_middle * modul[2]).astype(BF16)
    grad_gate_one = jnp.sum(grad_middle * attn_branch, axis=0)
    grad_heads = jnp.einsum(
        "td,de->te", grad_attn, weights[3], preferred_element_type=F32
    ).astype(BF16)
    grad_parts = attend_backward(
        *arranged, key_mask, softmax_stats, split_heads(grad_heads, length)
    )
    grad_qkv = jnp.stack([part.reshape(tokens, width) for part in grad_parts])
    grad_hidden_one = jnp.einsum(
        "kte,kde->td", grad_qkv, weights[0:3], preferred_element_type=F32
    )
    grad_norm_one, grad_shift_one, grad_scale_one = norm_backward(
        grad_hidden_one, normed_one, inverse_one, modul[1]
    )
    grad_input = grad_middle + grad_norm_one
    operands = (
        hidden_one,
        grad_qkv,
        grad_attn,
        heads_out,
        hidden_two,
        grad_upper,
        grad_mlp,
        active,
    )
    grad_modul = jnp.stack(
        [
            grad_shift_one,
            grad_scale_one,
            grad_gate_one,
            grad_shift_two,
            grad_scale_two,
            grad_gate_two,
        ]
    )
    qkv_sums = jnp.sum(grad_qkv, axis=1, dtype=F32)
    grad_lin = jnp.concatenate(
        [
            qkv_sums[0:1],
            qkv_sums[2:3],
            jnp.sum(grad_attn, axis=0, dtype=F32)[None],
            jnp.sum(grad_upper, axis=1, dtype=F32),
            jnp.sum(grad_mlp, axis=0, dtype=F32)[None],
        ],
        axis=0,
    )
    return (grad_input, grad_modul, grad_lin, operands)


def on_device(
    block_input,
    condition,
    frame_counts,
    cotangent,
    qkv_weight,
    qkv_first,
    qkv_second,
    out_weight,
    out_first,
    out_second,
    up_weight,
    up_first,
    up_second,
    down_weight,
    down_first,
    down_second,
    ada_weight,
    ada_first,
    ada_second,
    bias_weight,
    bias_first,
    bias_second,
):
    wide_count = lax.axis_size("wide")
    narrow_count = lax.axis_size("narrow")
    wide_at = lax.axis_index("wide")
    narrow_at = lax.axis_index("narrow")
    frames = block_input.shape[0] // PATCHES
    clip_total = condition.shape[0]
    col_width = block_input.shape[1]
    rows_tile = qkv_weight.shape[1]
    expand = up_weight.shape[2]
    full_width = col_width * narrow_count
    col_start = narrow_at * col_width
    clip_devices = 2 * narrow_count
    own_frames = frames // narrow_count
    own_patches = PATCHES // clip_devices
    own_tokens = own_frames * PATCHES
    clip_at = wide_at // 2

    silu_cond = jax.nn.silu(condition)
    cond_rows = lax.dynamic_slice_in_dim(silu_cond, wide_at * rows_tile, rows_tile, 1)
    partial_mod = jnp.einsum("cd,ldke->lcke", cond_rows, ada_weight, precision=HIGHEST_PREC)
    ada_bias = bias_weight[:, 4 + expand : 10 + expand]
    here = (wide_at == 0).astype(F32)
    partial_mod = partial_mod + here * ada_bias[:, None]
    lin_rows = 4 + expand
    packed = jnp.concatenate(
        [
            partial_mod.reshape(2, clip_total * 6, col_width),
            here * bias_weight[:, :lin_rows],
        ],
        axis=1,
    )
    zero_at = jnp.zeros((), jnp.int32)
    padded = lax.dynamic_update_slice(
        jnp.zeros((2, clip_total * 6 + lin_rows, full_width), F32),
        packed,
        (zero_at, zero_at, col_start),
    )
    vectors = lax.psum(padded, ("wide", "narrow"))
    modul = lax.dynamic_slice_in_dim(vectors, clip_at * 6, 6, 1)
    lin_bias = vectors[:, clip_total * 6 :]

    tiles = jnp.concatenate(
        [
            jnp.transpose(qkv_weight.astype(BF16), (0, 2, 1, 3)),
            out_weight.astype(BF16)[:, None],
            jnp.transpose(up_weight.astype(BF16), (0, 2, 1, 3)),
            jnp.transpose(down_weight.astype(BF16), (0, 2, 1, 3)),
        ],
        axis=1,
    )
    per = KINDS // narrow_count
    tiles = jnp.transpose(
        tiles.reshape(2, narrow_count, per, rows_tile, col_width), (1, 0, 2, 3, 4)
    )
    inputs_by_frame = block_input.astype(BF16).reshape(narrow_count, own_tokens, col_width)
    cot_by_patch = jnp.transpose(
        cotangent.astype(BF16).reshape(frames, clip_devices, own_patches, col_width), (1, 0, 2, 3)
    )
    tiles, inputs_by_frame, cot_by_patch = swap((tiles, inputs_by_frame, cot_by_patch), 0, "swap_in")
    own = jnp.transpose(tiles, (1, 2, 3, 0, 4)).reshape(2, per, rows_tile, full_width)
    weights = gather_weights(own, 1)

    residual = (
        jnp.transpose(inputs_by_frame, (1, 0, 2)).reshape(own_tokens, full_width).astype(F32)
    )
    grad_state = (
        jnp.transpose(
            cot_by_patch.reshape(2, narrow_count, frames, own_patches, col_width), (3, 0, 2, 1, 4)
        )
        .reshape(own_tokens, full_width)
        .astype(F32)
    )

    group = 128
    own_count = lax.dynamic_slice_in_dim(frame_counts, clip_at, 1, 0)[0]
    places_in = jnp.arange(group, dtype=jnp.int32)
    temporal_mask = jnp.logical_and(
        places_in[:, None] // CLIP_LEN == places_in[None, :] // CLIP_LEN,
        (places_in % CLIP_LEN < own_count)[None, :],
    )

    state, kept_spatial = forward_block(
        residual, modul[0], weights[0], lin_bias[0], PATCHES, None
    )
    by_patch = jnp.transpose(
        state.astype(BF16).reshape(own_frames, clip_devices, own_patches, full_width), (1, 0, 2, 3)
    )
    (by_patch,) = swap((by_patch,), 2, "swap_to_patches")
    state = (
        jnp.transpose(by_patch, (2, 0, 1, 3)).reshape(own_tokens, full_width).astype(F32)
    )
    state, kept_temporal = forward_block(
        state, modul[1], weights[1], lin_bias[1], group, temporal_mask
    )
    out_pieces = jnp.transpose(
        state.astype(BF16).reshape(own_patches, 2, frames, narrow_count, col_width),
        (1, 3, 2, 0, 4),
    ).reshape(clip_devices, frames, own_patches, col_width)

    grad_state, grad_modul_t, grad_lin_t, grads_t = backward_block(
        grad_state, kept_temporal, modul[1], weights[1], group, temporal_mask
    )
    by_frame = jnp.transpose(
        grad_state.astype(BF16).reshape(own_patches, clip_devices, own_frames, full_width),
        (1, 2, 0, 3),
    )
    (by_frame,) = swap((by_frame,), 3, "swap_to_frames")
    grad_state = (
        jnp.transpose(by_frame, (1, 0, 2, 3)).reshape(own_tokens, full_width).astype(F32)
    )
    grad_state, grad_modul_s, grad_lin_s, grads_s = backward_block(
        grad_state, kept_spatial, modul[0], weights[0], PATCHES, None
    )
    in_pieces = jnp.transpose(
        grad_state.astype(BF16).reshape(own_tokens, narrow_count, col_width), (1, 0, 2)
    )
    tile_grads, (out_pieces, in_pieces) = scatter_grads(
        grads_t + grads_s, (out_pieces, in_pieces), rows_tile, 4
    )
    block_output = (
        jnp.transpose(out_pieces, (1, 0, 2, 3)).astype(F32).reshape(frames * PATCHES, col_width)
    )
    input_grad = in_pieces.astype(F32).reshape(frames * PATCHES, col_width)

    tile_grads = tile_grads.astype(F32)
    vector_grads = jnp.concatenate(
        [
            lax.dynamic_update_slice(
                jnp.zeros((2, clip_total * 6, full_width), F32),
                jnp.stack([grad_modul_s, grad_modul_t]),
                (zero_at, clip_at * 6, zero_at),
            ),
            jnp.stack([grad_lin_s, grad_lin_t]),
        ],
        axis=1,
    )
    vector_grads = lax.dynamic_slice_in_dim(
        lax.psum(vector_grads, ("wide", "narrow")), col_start, col_width, 2
    )
    grad_clip_mod = vector_grads[:, : clip_total * 6].reshape(2, clip_total, 6, col_width)
    grad_lin = vector_grads[:, clip_total * 6 :]

    grad_ada = jnp.einsum("cd,lcke->ldke", cond_rows, grad_clip_mod, precision=HIGHEST_PREC)
    grad_bias = jnp.concatenate([grad_lin, jnp.sum(grad_clip_mod, axis=1)], axis=1)
    by_rows = lambda part: jnp.transpose(part, (0, 2, 1, 3))
    gradients = (
        by_rows(tile_grads[:, 0:3]),
        tile_grads[:, 3],
        by_rows(tile_grads[:, 4 : 4 + expand]),
        by_rows(tile_grads[:, 4 + expand :]),
        grad_ada,
        grad_bias,
    )
    masters = (qkv_weight, out_weight, up_weight, down_weight, ada_weight, bias_weight)
    firsts = (qkv_first, out_first, up_first, down_first, ada_first, bias_first)
    seconds = (qkv_second, out_second, up_second, down_second, ada_second, bias_second)
    shares = (1.0, 1.0, 1.0, 1.0, 1.0, 1.0 / wide_count)
    local_sq = jnp.zeros((), F32)
    for gradient, share_of in zip(gradients, shares):
        local_sq = local_sq + jnp.sum(gradient * gradient) * share_of
    grad_norm = jnp.sqrt(lax.psum(local_sq, ("wide", "narrow")))
    factor = jnp.minimum(1.0, CLIP_LIMIT / grad_norm)
    first_fix = 1.0 - BETA_ONE**STEP
    second_fix = 1.0 - BETA_TWO**STEP
    updates = []
    states = []
    norm_terms = []
    for master, first_in, second_in, gradient, share_of in zip(
        masters, firsts, seconds, gradients, shares
    ):
        clipped = gradient * factor
        moment = BETA_ONE * first_in + (1.0 - BETA_ONE) * clipped
        square = BETA_TWO * second_in + (1.0 - BETA_TWO) * clipped * clipped
        update = (
            moment / first_fix / (jnp.sqrt(square / second_fix) + ADAM_EPS) + WEIGHT_DECAY * master
        )
        updates.append(update)
        states.append((moment, square))
        norm_terms.append(
            jnp.stack(
                [
                    jnp.sum((master * master).reshape(2, -1), axis=1),
                    jnp.sum((update * update).reshape(2, -1), axis=1),
                ],
                axis=1,
            )
            * share_of
        )
    trust_norms = jnp.sqrt(lax.psum(jnp.stack(norm_terms, axis=1), ("wide", "narrow")))
    trust_ratio = trust_norms[:, :, 0] / trust_norms[:, :, 1]
    results = []
    for position in range(6):
        master = masters[position]
        ratio_here = trust_ratio[:, position].reshape((2,) + (1,) * (master.ndim - 1))
        results.append(master - LEARN_RATE * ratio_here * updates[position])
        results.extend(states[position])
    return (block_output, input_grad, *results, trust_norms, grad_norm.reshape(1))


def solution(mesh):
    tokens = P("wide", "narrow")
    tall = P(None, "wide", None, "narrow")
    flat = P(None, "wide", "narrow")
    bias = P(None, None, "narrow")
    params = (tall,) * 3 + (flat,) * 3 + (tall,) * 9 + (bias,) * 3
    return jax.shard_map(
        on_device,
        mesh=mesh,
        in_specs=(tokens, P(), P(), tokens) + params,
        out_specs=(tokens, tokens) + params + (P(), P()),
        check_vma=False,
    )
```
